32 devices in a mesh: grp: 8 (over z, core), blk: 4 (over y, x).
Axes of the slice: x: 2, y: 2, z: 4, core: 2. Of those that a mesh axis runs over, the one named last changes fastest.
Arguments:
- solid_fraction: float32 [192, 32, 2048], P('grp', 'blk'), may hold values from 0.2 to 1
- thermal_state: float32 [192, 32, 2048], P('grp', 'blk'), may hold values from -6 to 6
- target_heat_sensitivity: float32 [192, 32, 2048], P('grp', 'blk'), may hold values from -6 to 6
- coolant_coupling: float32 [192, 32, 2048], P('grp', 'blk'), may hold values from 0.25 to 2
- design_switch: int32 [8, 4, 8], P('grp', 'blk'), may hold values from 0 to 1, as said below
Outputs:
- sensitivity: float32 [192, 32, 2048], P('grp', 'blk')
The draws below stay inside these ranges and needn't reach their ends.
Inputs may be any that keep to these rules, and one draw needn't show every extreme that they name: `design_switch`: every device's 8 blocks hold at least one active block, and on some device all 8 are active.
All inputs are finite; a program needn't handle non-finite values.
Results may differ from the reference program's by a relative error of at most 0.0001.
Values sent between devices are 32-bit elements; how exact they have to be, the bound alone decides.
A program may use at most 128 MiB of HBM per device.

```python
import math
import jax
import jax.numpy as jnp
from jax import lax

GRID_LENGTH_Z = 2048
BX = 256
RADIUS = 48
SWEEPS = 4
GRID_LENGTH_X = 192
GRID_LENGTH_Y = 32
NBX = 8
ZBLOCKS = 8
YBLOCKS = 4


def draw_design_switch(key, part):
    key_counts, key_full, key_order = jax.random.split(key, 3)
    devices_total = ZBLOCKS * YBLOCKS
    counts = jax.random.randint(key_counts, (devices_total,), 1, NBX + 1)
    full_device = jax.random.randint(key_full, (), 0, devices_total)
    counts = jnp.where(jnp.arange(devices_total) == full_device, NBX, counts)
    orders = jax.vmap(lambda single: jax.random.permutation(single, NBX))(jax.random.split(key_order, devices_total))
    marks = (orders < counts[:, None]).astype(jnp.int32)
    return marks.reshape(ZBLOCKS, YBLOCKS, NBX)


def steps_of(key, shape, pieces, low, high):
    loudness = 1.0
    for position, blocks in pieces:
        heights = jax.random.uniform(jax.random.fold_in(jax.random.fold_in(key, 6), position), (blocks,), jnp.float32, low / len(pieces), high / len(pieces))
        loudness = loudness * jnp.repeat(jnp.exp(heights), shape[position] // blocks).reshape((-1,) + (1,) * (len(shape) - 1 - position))
    return loudness


def gaussian(key, shape, scale, reach, cuts=(), kind=jnp.bfloat16):
    loudness = steps_of(key, shape, cuts, -0.22, 0.18) if cuts else 1.0
    array = jax.random.normal(key, shape, jnp.float32) * scale * loudness
    return jnp.minimum(jnp.maximum(array, -reach), reach).astype(kind)


def setup_inputs(seed: int = 0) -> dict:
    seeds = jax.random.split(jax.random.key(seed), 6)
    return {
        "solid_fraction": jnp.clip(0.2 + 0.8 * jax.random.uniform(seeds[0], (GRID_LENGTH_X, GRID_LENGTH_Y, GRID_LENGTH_Z), jnp.float32) ** steps_of(seeds[0], (GRID_LENGTH_X, GRID_LENGTH_Y, GRID_LENGTH_Z), ((0, 8), (1, 4)), -0.2, 0.2), 0.2, 1.0),
        "thermal_state": gaussian(seeds[1], (GRID_LENGTH_X, GRID_LENGTH_Y, GRID_LENGTH_Z), 1.0, 6.0, ((0, 8), (1, 4)), jnp.float32),
        "target_heat_sensitivity": gaussian(seeds[2], (GRID_LENGTH_X, GRID_LENGTH_Y, GRID_LENGTH_Z), 1.0, 6.0, ((0, 8), (1, 4)), jnp.float32),
        "coolant_coupling": jnp.clip(jnp.exp(math.log(2.0) - 2.0794415 * jax.random.uniform(seeds[3], (GRID_LENGTH_X, GRID_LENGTH_Y, GRID_LENGTH_Z), jnp.float32) ** steps_of(seeds[3], (GRID_LENGTH_X, GRID_LENGTH_Y, GRID_LENGTH_Z), ((0, 8), (1, 4)), -0.2, 0.2)), 0.25, 2.0),
        "design_switch": draw_design_switch(jax.random.fold_in(seeds[5], 71), 0),
    }


COND_FLOOR = 0.001
DAMPING_WEIGHT = 2.0 / 3.0
REPORT_SCALE = 100.0


def cone_weight(distance):
    return jnp.maximum(RADIUS + 1 - jnp.abs(distance), 0).astype(jnp.float32)


def coverage(positions, length):
    offsets = jnp.arange(-RADIUS, RADIUS + 1, dtype=jnp.int32)
    reached = positions[:, None] + offsets[None, :]
    inside = (reached >= 0) & (reached < length)
    return jnp.sum(jnp.where(inside, cone_weight(offsets)[None, :], jnp.float32(0.0)), axis=1)


def nearby_voxels(padded):
    return [padded[2:, 1:-1, 1:-1], padded[:-2, 1:-1, 1:-1],
            padded[1:-1, 2:, 1:-1], padded[1:-1, :-2, 1:-1],
            padded[1:-1, 1:-1, 2:], padded[1:-1, 1:-1, :-2]]


def apply_mask(values, design_switch):
    depth = values.shape[0] // design_switch.shape[0]
    span = values.shape[1] // design_switch.shape[1]
    shaped = values.reshape(design_switch.shape[0], depth, design_switch.shape[1], span, design_switch.shape[2], BX)
    gating = design_switch.astype(jnp.float32)[:, None, :, None, :, None]
    return (shaped * gating).reshape(values.shape)


def filter_x(values):
    extent = values.shape[2]
    count_blocks = extent // BX
    scaled = values / coverage(jnp.arange(extent, dtype=jnp.int32), extent)[None, None, :]
    blocks = scaled.reshape(-1, count_blocks, BX)
    padded = jnp.pad(blocks, ((0, 0), (1, 1), (0, 0)))
    positions = jnp.arange(BX, dtype=jnp.int32)
    result_sum = jnp.zeros(blocks.shape, jnp.float32)
    for block_step in (-1, 0, 1):
        weights_table = cone_weight(block_step * BX + positions[:, None] - positions[None, :])
        result_sum = result_sum + jnp.einsum("rbi,ij->rbj", padded[:, 1 + block_step:1 + block_step + count_blocks], weights_table, precision=lax.Precision.HIGHEST)
    return result_sum.reshape(values.shape)


def filter_y(values):
    extent = values.shape[1]
    positions = jnp.arange(extent, dtype=jnp.int32)
    scaled = values / coverage(positions, extent)[None, :, None]
    weights_table = cone_weight(positions[:, None] - positions[None, :])
    return jnp.einsum("zyx,yw->zwx", scaled, weights_table, precision=lax.Precision.HIGHEST)


def filter_z(values):
    extent = values.shape[0]
    positions = jnp.arange(extent, dtype=jnp.int32)
    scaled = values / coverage(positions, extent)[:, None, None]
    weights_table = cone_weight(positions[:, None] - positions[None, :])
    return jnp.einsum("zyx,zw->wyx", scaled, weights_table, precision=lax.Precision.HIGHEST)


def reference(solid_fraction, thermal_state, target_heat_sensitivity, coolant_coupling, design_switch):
    interface_flux_factor = COND_FLOOR + (1.0 - COND_FLOOR) * solid_fraction ** 3
    face_conduct = [0.5 * (interface_flux_factor + beside) for beside in nearby_voxels(jnp.pad(interface_flux_factor, 1))]
    matrix_main_entry = coolant_coupling + sum(face_conduct)
    lagrange_multiplier = target_heat_sensitivity / matrix_main_entry
    for iteration in range(SWEEPS):
        incoming_flux = sum(weight_face * beside for weight_face, beside in zip(face_conduct, nearby_voxels(jnp.pad(lagrange_multiplier, 1))))
        lagrange_multiplier = lagrange_multiplier + DAMPING_WEIGHT * (target_heat_sensitivity - matrix_main_entry * lagrange_multiplier + incoming_flux) / matrix_main_entry
    couple_multiplied = sum((lagrange_multiplier - nearby_multiplier) * (thermal_state - nearby_heat_level)
                   for nearby_multiplier, nearby_heat_level in zip(nearby_voxels(jnp.pad(lagrange_multiplier, 1)), nearby_voxels(jnp.pad(thermal_state, 1))))
    stiff_slope = 3.0 * (1.0 - COND_FLOOR) * solid_fraction ** 2
    raw = apply_mask(-0.5 * couple_multiplied * stiff_slope, design_switch)
    along_z = filter_z(filter_y(filter_x(raw)))
    return apply_mask(REPORT_SCALE * along_z, design_switch)
```

```python
import functools

import jax
import jax.numpy as jnp
from jax import lax
from jax.experimental import pallas as pl
from jax.experimental.pallas import tpu as pltpu
from jax.sharding import PartitionSpec as P

BX = 256
RADIUS = 48
SWEEPS = 4
COND_FLOOR = 0.001
REPORT_SCALE = 100.0
GROUP = 8

MESH = pl.DeviceIdType.MESH
F32 = jnp.float32


def coverage(position, length):
    low = jnp.maximum(RADIUS - position, 0)
    high = jnp.maximum(RADIUS - (length - 1 - position), 0)
    lost = low * (low + 1) // 2 + high * (high + 1) // 2
    return ((RADIUS + 1) ** 2 - lost).astype(F32)


def kernel(n_grp, n_blk, near, far, *refs):
    (
        solid_hbm, temp_hbm, target_hbm, coupling_hbm, switch,
        out,
        solid, temp, target, coupling, cond, adj, third, fixed, raw, filt,
        y_send, y_recv, mom_send, mom_recv, zmom_send, zmom_recv, far_z,
        mask, scale, z_inv, padded, cone,
        load_sem, y_ssem, y_rsem, z_ssem, z_rsem,
        mom_ssem, mom_rsem, zm_ssem, zm_rsem, fz_ssem, fz_rsem,
    ) = refs[:39]
    depth, span, extent = solid.shape
    groups = depth // GROUP
    grp = lax.axis_index("grp")
    blk = lax.axis_index("blk")
    reach = max(near + far)

    def has(axis, step):
        if axis == "grp":
            at, count = grp + step, n_grp
        else:
            at, count = blk + step, n_blk
        return (at < count) if step > 0 else (at >= 0)

    def peer(axis, step):
        return {axis: (grp if axis == "grp" else blk) + step}

    partners = [("grp", s * d) for d in (1, 2) for s in (1, -1) if d < n_grp]
    partners += [("blk", s * d) for d in near + far for s in (1, -1)]

    loads = [
        pltpu.make_async_copy(solid_hbm, solid, load_sem.at[0]),
        pltpu.make_async_copy(temp_hbm, temp.at[pl.ds(1, depth)], load_sem.at[1]),
        pltpu.make_async_copy(target_hbm, target, load_sem.at[2]),
        pltpu.make_async_copy(coupling_hbm, coupling, load_sem.at[3]),
    ]
    for load in loads:
        load.start()

    barrier = pltpu.get_barrier_semaphore()
    total = 0
    for axis, step in partners:
        total = total + has(axis, step).astype(jnp.int32)

        @pl.when(has(axis, step))
        def _(axis=axis, step=step):
            pl.semaphore_signal(
                barrier, inc=1, device_id=peer(axis, step), device_id_type=MESH
            )

    for side, step in ((0, -1), (1, 1)):
        edge = 0 if side == 0 else depth + 1

        @pl.when(jnp.logical_not(has("grp", step)))
        def _(side=side, edge=edge):
            zero = jnp.zeros((span, extent), F32)
            cond[edge] = zero
            temp[edge] = zero
            for s in range(SWEEPS + 1):
                adj[s, edge] = zero
            zmom_recv[side] = jnp.zeros((2, span, extent), F32)

        @pl.when(jnp.logical_not(has("grp", 2 * step)))
        def _(side=side):
            far_z[side] = jnp.zeros((depth, span, extent), F32)

        @pl.when(jnp.logical_not(has("blk", step)))
        def _(side=side):
            for item in range(SWEEPS + 3):
                y_recv[item, side] = jnp.zeros((depth, extent), F32)

        for k, d in enumerate(near):

            @pl.when(jnp.logical_not(has("blk", d * step)))
            def _(side=side, k=k):
                mom_recv[k, side] = jnp.zeros((2, depth, extent), F32)

        for k, d in enumerate(far):

            @pl.when(jnp.logical_not(has("blk", d * step)))
            def _(side=side, k=k):
                refs[39][k, side] = jnp.zeros((depth, span, extent), F32)

    row = lax.broadcasted_iota(jnp.int32, (span, extent), 0)
    lane = lax.broadcasted_iota(jnp.int32, (span, extent), 1)
    row_f = row.astype(F32)

    for b in range(extent // BX):
        mask[:, b * BX : (b + 1) * BX] = jnp.full(
            (span, BX), switch[0, 0, b].astype(F32), F32
        )
    scale[...] = (
        mask[...]
        * (-1.5 * (1.0 - COND_FLOOR))
        / (coverage(lane, extent) * coverage(row + blk * span, span * n_blk))
    )
    z_inv[...] = 1.0 / coverage(
        lax.broadcasted_iota(jnp.int32, (depth, extent), 0) + grp * depth, depth * n_grp
    )
    cone[...] = jnp.maximum(
        RADIUS
        + 1
        - jnp.abs(
            lax.broadcasted_iota(jnp.int32, (2 * BX, BX), 0)
            - BX // 2
            - lax.broadcasted_iota(jnp.int32, (2 * BX, BX), 1)
        ),
        0,
    ).astype(F32).astype(jnp.bfloat16)
    padded[:, :, : BX // 2] = jnp.zeros((depth, span, BX // 2), F32)
    padded[:, :, extent + BX // 2 :] = jnp.zeros((depth, span, BX // 2), F32)

    def remote(src, dst, ssem, rsem, axis, step):
        return pltpu.make_async_remote_copy(
            src_ref=src, dst_ref=dst, send_sem=ssem, recv_sem=rsem,
            device_id=peer(axis, step), device_id_type=MESH,
        )

    def y_copy(item, g, side):
        rows = pl.ds(g * GROUP, GROUP)
        return remote(
            y_send.at[item, side, rows], y_recv.at[item, side, rows],
            y_ssem.at[item, g, side], y_rsem.at[item, g, side],
            "blk", 1 if side == 0 else -1,
        )

    def z_copy(item, buf, side):
        src, dst = (depth, 0) if side == 0 else (1, depth + 1)
        return remote(
            buf.at[src], buf.at[dst], z_ssem.at[item, side], z_rsem.at[item, side],
            "grp", 1 if side == 0 else -1,
        )

    def mom_copy(k, g, side):
        rows = pl.ds(g * GROUP, GROUP)
        return remote(
            mom_send.at[:, rows], mom_recv.at[k, side, :, rows],
            mom_ssem.at[k, g, side], mom_rsem.at[k, g, side],
            "blk", near[k] if side == 0 else -near[k],
        )

    def far_y_copy(k, g, side):
        rows = pl.ds(g * GROUP, GROUP)
        return remote(
            raw.at[rows], refs[39].at[k, side, rows],
            refs[40].at[k, g, side], refs[41].at[k, g, side],
            "blk", far[k] if side == 0 else -far[k],
        )

    def far_z_copy(g, side):
        rows = pl.ds(g * GROUP, GROUP)
        return remote(
            filt.at[rows], far_z.at[side, rows], fz_ssem.at[g, side], fz_rsem.at[g, side],
            "grp", 2 if side == 0 else -2,
        )

    def zmom_copy(side):
        return remote(
            zmom_send, zmom_recv.at[side], zm_ssem.at[side], zm_rsem.at[side],
            "grp", 1 if side == 0 else -1,
        )

    def both(make, axis, step, act):
        for side, sign in ((0, 1), (1, -1)):
            where = has(axis, -sign * step) if act == "come" else has(axis, sign * step)

            @pl.when(where)
            def _(side=side):
                copy = make(side)
                if act == "start":
                    copy.start()
                elif act == "sent":
                    copy.wait_send()
                else:
                    copy.wait_recv()

    def one(make, axis, step, side, act):
        sign = 1 if side == 0 else -1
        where = has(axis, -sign * step) if act == "come" else has(axis, sign * step)

        @pl.when(where)
        def _():
            copy = make(side)
            if act == "start":
                copy.start()
            elif act == "sent":
                copy.wait_send()
            else:
                copy.wait_recv()

    def x_shift(v):
        low = jnp.where(lane == 0, 0.0, pltpu.roll(v, 1, 1))
        high = jnp.where(lane == extent - 1, 0.0, pltpu.roll(v, extent - 1, 1))
        return low, high

    def y_shift(v, low_row, high_row):
        low = jnp.where(row == 0, low_row, pltpu.roll(v, 1, 0))
        high = jnp.where(row == span - 1, high_row, pltpu.roll(v, span - 1, 0))
        return low, high

    def halo(item, z):
        return y_recv[item, 0, pl.ds(z, 1), :], y_recv[item, 1, pl.ds(z, 1), :]

    def put_rows(item, z, v):
        y_send[item, 0, pl.ds(z, 1), :] = v[span - 1 : span]
        y_send[item, 1, pl.ds(z, 1), :] = v[0:1]

    def layers(g, body):
        @pl.loop(g * GROUP, (g + 1) * GROUP)
        def _(z):
            body(z)

    loads[0].wait()
    loads[1].wait()

    def conductivity(z):
        s = solid[z]
        c = COND_FLOOR + (1.0 - COND_FLOOR) * (s * s * s)
        cond[z + 1] = c
        put_rows(0, z, c)
        put_rows(1, z, temp[z + 1])

    pl.semaphore_wait(barrier, total)
    for g in range(groups):
        layers(g, conductivity)
        both(functools.partial(y_copy, 0, g), "blk", 1, "start")
        if g == 0:
            one(functools.partial(z_copy, 0, cond), "grp", 1, 1, "start")
    one(functools.partial(z_copy, 0, cond), "grp", 1, 0, "start")
    loads[2].wait()
    loads[3].wait()

    def start_adjoint(z):
        c = cond[z + 1]
        low_row, high_row = halo(0, z)
        xl, xh = x_shift(c)
        yl, yh = y_shift(c, low_row, high_row)
        near_sum = (cond[z] + cond[z + 2]) + (xl + xh) + (yl + yh)
        inverse = 1.0 / (coupling[z] + 3.0 * c + 0.5 * near_sum)
        a = target[z] * inverse
        third[z] = inverse * (1.0 / 3.0)
        fixed[z] = a * (2.0 / 3.0)
        adj[0, z + 1] = a
        put_rows(2, z, a)

    def sweep(s, z):
        c = cond[z + 1]
        a = adj[s, z + 1]
        cl, ch = halo(0, z)
        al, ah = halo(s + 2, z)
        ca = c * a
        axl, axh = x_shift(a)
        gxl, gxh = x_shift(ca)
        ayl, ayh = y_shift(a, al, ah)
        gyl, gyh = y_shift(ca, cl * al, ch * ah)
        below, above = adj[s, z], adj[s, z + 2]
        plain = (below + above) + (axl + axh) + (ayl + ayh)
        weighted = (cond[z] * below + cond[z + 2] * above) + (gxl + gxh) + (gyl + gyh)
        new = a * (1.0 / 3.0) + fixed[z] + third[z] * (c * plain + weighted)
        adj[s + 1, z + 1] = new
        put_rows(s + 3, z, new)

    def raw_terms(z):
        a = adj[SWEEPS, z + 1]
        t = temp[z + 1]
        al, ah = halo(SWEEPS + 2, z)
        tl, th = halo(1, z)
        axl, axh = x_shift(a)
        txl, txh = x_shift(t)
        ayl, ayh = y_shift(a, al, ah)
        tyl, tyh = y_shift(t, tl, th)
        total_terms = (
            (a - adj[SWEEPS, z]) * (t - temp[z])
            + (a - adj[SWEEPS, z + 2]) * (t - temp[z + 2])
            + (a - axl) * (t - txl)
            + (a - axh) * (t - txh)
            + (a - ayl) * (t - tyl)
            + (a - ayh) * (t - tyh)
        )
        s = solid[z]
        value = total_terms * (s * s) * scale[...] * z_inv[pl.ds(z, 1), :]
        raw[z] = value
        mom_send[0, pl.ds(z, 1), :] = jnp.sum(value, axis=0, keepdims=True)
        mom_send[1, pl.ds(z, 1), :] = jnp.sum(value * row_f, axis=0, keepdims=True)

    def stage(item, buf, body, wait_item, wait_buf, after):
        for g in range(groups):
            both(functools.partial(y_copy, wait_item, g), "blk", 1, "come")
            if wait_item == SWEEPS + 2:
                both(functools.partial(y_copy, 1, g), "blk", 1, "come")
            if g == 0:
                one(functools.partial(z_copy, wait_item, wait_buf), "grp", 1, 0, "come")
                if wait_item == SWEEPS + 2:
                    one(functools.partial(z_copy, 1, temp), "grp", 1, 0, "come")
            if g == groups - 1:
                one(functools.partial(z_copy, wait_item, wait_buf), "grp", 1, 1, "come")
                if wait_item == SWEEPS + 2:
                    one(functools.partial(z_copy, 1, temp), "grp", 1, 1, "come")
            layers(g, body)
            if item is None:
                after(g)
            else:
                both(functools.partial(y_copy, item, g), "blk", 1, "start")
                if g == 0:
                    one(functools.partial(z_copy, item, buf), "grp", 1, 1, "start")
        if item is not None:
            one(functools.partial(z_copy, item, buf), "grp", 1, 0, "start")

    stage(2, adj.at[0], start_adjoint, 0, cond, None)
    for g in range(groups):
        both(functools.partial(y_copy, 1, g), "blk", 1, "start")
    both(functools.partial(z_copy, 1, temp), "grp", 1, "start")
    for s in range(SWEEPS):
        stage(s + 3, adj.at[s + 1], functools.partial(sweep, s), s + 2, adj.at[s], None)

    def send_moments(g):
        for k, d in enumerate(near):
            both(functools.partial(mom_copy, k, g), "blk", d, "start")
        for k, d in enumerate(far):
            both(functools.partial(far_y_copy, k, g), "blk", d, "start")

    stage(None, None, raw_terms, SWEEPS + 2, adj.at[SWEEPS], send_moments)

    zmom_send[...] = jnp.zeros((2, span, extent), F32)

    def along_y(z):
        level = jnp.zeros((1, extent), F32)
        slope = jnp.zeros((1, extent), F32)
        for k, d in enumerate(near):
            weight = float(RADIUS + 1 - span * d)
            low0, low1 = mom_recv[k, 0, 0, pl.ds(z, 1), :], mom_recv[k, 0, 1, pl.ds(z, 1), :]
            high0, high1 = mom_recv[k, 1, 0, pl.ds(z, 1), :], mom_recv[k, 1, 1, pl.ds(z, 1), :]
            level = level + weight * (low0 + high0) + (low1 - high1)
            slope = slope + (high0 - low0)
        value = level + slope * row_f
        here = raw[z]
        for i in range(span):
            value = value + (RADIUS + 1 - jnp.abs(row - i)).astype(F32) * here[i : i + 1]
        for k, d in enumerate(far):
            low, high = refs[39][k, 0, z], refs[39][k, 1, z]
            for i in range(span):
                w_low = jnp.maximum(RADIUS + 1 - (span * d + row - i), 0).astype(F32)
                w_high = jnp.maximum(RADIUS + 1 - (span * d + i - row), 0).astype(F32)
                value = value + w_low * low[i : i + 1] + w_high * high[i : i + 1]
        filt[z] = value
        zmom_send[0] += value
        zmom_send[1] += value * jnp.asarray(z, F32)

    for g in range(groups):
        for k, d in enumerate(near):
            both(functools.partial(mom_copy, k, g), "blk", d, "come")
        for k, d in enumerate(far):
            both(functools.partial(far_y_copy, k, g), "blk", d, "come")
        layers(g, along_y)
        both(functools.partial(far_z_copy, g), "grp", 2, "start")
    both(zmom_copy, "grp", 1, "start")
    both(zmom_copy, "grp", 1, "come")
    for g in range(groups):
        both(functools.partial(far_z_copy, g), "grp", 2, "come")

    width = 512

    @pl.loop(0, extent // width)
    def _(b):
        cols = pl.ds(pl.multiple_of(b * width, width), width)
        shifted = pl.ds(pl.multiple_of(b * width + BX // 2, 128), width)
        own0, own1 = zmom_send[0, :, cols], zmom_send[1, :, cols]
        low0, low1 = zmom_recv[0, 0, :, cols], zmom_recv[0, 1, :, cols]
        high0, high1 = zmom_recv[1, 0, :, cols], zmom_recv[1, 1, :, cols]
        weight = float(RADIUS + 1 - depth)
        level = (RADIUS + 1.0) * own0 - own1 + weight * (low0 + high0) + low1 - high1
        slope = own0 - low0 + high0
        zero = jnp.zeros((span, width), F32)

        def up(z, carry):
            line, twice, once, far_twice, far_once = carry
            far_once = far_once + far_z[1, z, :, cols]
            far_twice = far_twice + far_once
            padded[z, :, shifted] = line - 2.0 * twice + far_twice
            once = once + filt[z, :, cols]
            return line + slope, twice + once, once, far_twice, far_once

        lax.fori_loop(0, depth, up, (level, zero, zero, zero, zero))

        def down(k, carry):
            far_twice, far_once = carry
            z = depth - 1 - k
            far_once = far_once + far_z[0, z, :, cols]
            far_twice = far_twice + far_once
            padded[z, :, shifted] += far_twice
            return far_twice, far_once

        lax.fori_loop(0, depth, down, (zero, zero))

    @pl.loop(0, extent // BX)
    def _(b):
        window = padded[:, :, pl.ds(pl.multiple_of(b * BX, BX), 2 * BX)]
        window = window.reshape(depth * span, 2 * BX)
        high = window.astype(jnp.bfloat16)
        low = (window - high.astype(F32)).astype(jnp.bfloat16)
        weights = cone[...]
        product = jnp.dot(high, weights, preferred_element_type=F32) + jnp.dot(
            low, weights, preferred_element_type=F32
        )
        cols = pl.ds(pl.multiple_of(b * BX, BX), BX)
        out[:, :, cols] = product.reshape(depth, span, BX) * (
            REPORT_SCALE * mask[:, cols]
        )

    for item in range(SWEEPS + 3):
        for g in range(groups):
            both(functools.partial(y_copy, item, g), "blk", 1, "sent")
        buf = (cond, temp)[item] if item < 2 else adj.at[item - 2]
        both(functools.partial(z_copy, item, buf), "grp", 1, "sent")
    for g in range(groups):
        for k, d in enumerate(near):
            both(functools.partial(mom_copy, k, g), "blk", d, "sent")
        for k, d in enumerate(far):
            both(functools.partial(far_y_copy, k, g), "blk", d, "sent")
        both(functools.partial(far_z_copy, g), "grp", 2, "sent")
    both(zmom_copy, "grp", 1, "sent")


def local(n_grp, n_blk, solid, temp, target, coupling, switch):
    depth, span, extent = solid.shape
    groups = depth // GROUP
    assert 2 * depth == RADIUS and depth % GROUP == 0
    near, far = [], []
    for d in range(1, n_blk):
        if (d + 1) * span - 1 <= RADIUS + 1:
            near.append(d)
        elif (d - 1) * span + 1 <= RADIUS:
            far.append(d)
    items = SWEEPS + 3
    block = (depth, span, extent)
    framed = (depth + 2, span, extent)
    vmem = lambda *shape: pltpu.VMEM(shape, F32)
    dma = lambda *shape: pltpu.SemaphoreType.DMA(shape)
    scratch = [
        vmem(*block), vmem(*framed), vmem(*block), vmem(*block),
        vmem(*framed), vmem(SWEEPS + 1, *framed), vmem(*block), vmem(*block),
        vmem(*block), vmem(*block),
        vmem(items, 2, depth, extent), vmem(items, 2, depth, extent),
        vmem(2, depth, extent), vmem(len(near), 2, 2, depth, extent),
        vmem(2, span, extent), vmem(2, 2, span, extent), vmem(2, *block),
        vmem(span, extent), vmem(span, extent), vmem(depth, extent),
        vmem(depth, span, extent + BX), pltpu.VMEM((2 * BX, BX), jnp.bfloat16),
        dma(4), dma(items, groups, 2), dma(items, groups, 2), dma(items, 2), dma(items, 2),
        dma(len(near), groups, 2), dma(len(near), groups, 2), dma(2), dma(2),
        dma(groups, 2), dma(groups, 2),
    ]
    if far:
        scratch += [
            vmem(len(far), 2, *block), dma(len(far), groups, 2), dma(len(far), groups, 2),
        ]
    return pl.pallas_call(
        functools.partial(kernel, n_grp, n_blk, near, far),
        out_shape=jax.ShapeDtypeStruct(block, F32),
        in_specs=[pl.BlockSpec(memory_space=pl.ANY)] * 4
        + [pl.BlockSpec(memory_space=pltpu.SMEM)],
        out_specs=pl.BlockSpec(memory_space=pltpu.VMEM),
        scratch_shapes=scratch,
        compiler_params=pltpu.CompilerParams(
            collective_id=0, has_side_effects=True, vmem_limit_bytes=60 * 2**20
        ),
        cost_estimate=pl.CostEstimate(
            flops=2 * 10**9, bytes_accessed=8 * 10**6, transcendentals=0
        ),
    )(solid, temp, target, coupling, switch)


def solution(mesh):
    spec = P("grp", "blk", None)
    return jax.shard_map(
        functools.partial(local, mesh.shape["grp"], mesh.shape["blk"]),
        mesh=mesh,
        in_specs=(spec,) * 5,
        out_specs=spec,
        check_vma=False,
    )
```

```python
import functools

import jax
import jax.numpy as jnp
from jax import lax
from jax.experimental import pallas as pl
from jax.experimental.pallas import tpu as pltpu
from jax.sharding import PartitionSpec as P

BX = 256
RADIUS = 48
SWEEPS = 4
COND_FLOOR = 0.001
REPORT_SCALE = 100.0
GROUP = 8

MESH = pl.DeviceIdType.MESH
F32 = jnp.float32


def coverage(position, length):
    low = jnp.maximum(RADIUS - position, 0)
    high = jnp.maximum(RADIUS - (length - 1 - position), 0)
    lost = low * (low + 1) // 2 + high * (high + 1) // 2
    return ((RADIUS + 1) ** 2 - lost).astype(F32)


def kernel(n_grp, n_blk, near, far, *refs):
    (
        solid_hbm, temp_hbm, target_hbm, coupling_hbm, switch,
        out,
        solid, temp, target, coupling, cond, adj, third, fixed, raw, filt,
        y_send, y_recv, mom_send, mom_recv, zmom_send, zmom_recv, far_z,
        mask, scale, z_inv, padded, cone,
        load_sem, y_ssem, y_rsem, z_ssem, z_rsem,
        mom_ssem, mom_rsem, zm_ssem, zm_rsem, fz_ssem, fz_rsem,
        passing, pass_ssem, pass_rsem, onward_ssem,
    ) = refs[:43]
    depth, span, extent = solid.shape
    groups = depth // GROUP
    grp = lax.axis_index("grp")
    blk = lax.axis_index("blk")
    reach = max(near + far)

    def has(axis, step):
        if axis == "grp":
            at, count = grp + step, n_grp
        else:
            at, count = blk + step, n_blk
        return (at < count) if step > 0 else (at >= 0)

    def peer(axis, step):
        return {axis: (grp if axis == "grp" else blk) + step}

    partners = [("grp", s * d) for d in (1, 2) for s in (1, -1) if d < n_grp]
    partners += [("blk", s * d) for d in near + far for s in (1, -1)]

    loads = [
        pltpu.make_async_copy(solid_hbm, solid, load_sem.at[0]),
        pltpu.make_async_copy(temp_hbm, temp.at[pl.ds(1, depth)], load_sem.at[1]),
        pltpu.make_async_copy(target_hbm, target, load_sem.at[2]),
        pltpu.make_async_copy(coupling_hbm, coupling, load_sem.at[3]),
    ]
    for load in loads:
        load.start()

    barrier = pltpu.get_barrier_semaphore()
    total = 0
    for axis, step in partners:
        total = total + has(axis, step).astype(jnp.int32)

        @pl.when(has(axis, step))
        def _(axis=axis, step=step):
            pl.semaphore_signal(
                barrier, inc=1, device_id=peer(axis, step), device_id_type=MESH
            )

    for side, step in ((0, -1), (1, 1)):
        edge = 0 if side == 0 else depth + 1

        @pl.when(jnp.logical_not(has("grp", step)))
        def _(side=side, edge=edge):
            zero = jnp.zeros((span, extent), F32)
            cond[edge] = zero
            temp[edge] = zero
            for s in range(SWEEPS + 1):
                adj[s, edge] = zero
            zmom_recv[side] = jnp.zeros((2, span, extent), F32)

        @pl.when(jnp.logical_not(has("grp", 2 * step)))
        def _(side=side):
            far_z[side] = jnp.zeros((depth, span, extent), F32)

        @pl.when(jnp.logical_not(has("blk", step)))
        def _(side=side):
            for item in range(SWEEPS + 3):
                y_recv[item, side] = jnp.zeros((depth, extent), F32)

        for k, d in enumerate(near):

            @pl.when(jnp.logical_not(has("blk", d * step)))
            def _(side=side, k=k):
                mom_recv[k, side] = jnp.zeros((2, depth, extent), F32)

        for k, d in enumerate(far):

            @pl.when(jnp.logical_not(has("blk", d * step)))
            def _(side=side, k=k):
                refs[43][k, side] = jnp.zeros((depth, span, extent), F32)

    row = lax.broadcasted_iota(jnp.int32, (span, extent), 0)
    lane = lax.broadcasted_iota(jnp.int32, (span, extent), 1)
    row_f = row.astype(F32)

    for b in range(extent // BX):
        mask[:, b * BX : (b + 1) * BX] = jnp.full(
            (span, BX), switch[0, 0, b].astype(F32), F32
        )
    scale[...] = (
        mask[...]
        * (-1.5 * (1.0 - COND_FLOOR))
        / (coverage(lane, extent) * coverage(row + blk * span, span * n_blk))
    )
    z_inv[...] = 1.0 / coverage(
        lax.broadcasted_iota(jnp.int32, (depth, extent), 0) + grp * depth, depth * n_grp
    )
    cone[...] = jnp.maximum(
        RADIUS
        + 1
        - jnp.abs(
            lax.broadcasted_iota(jnp.int32, (2 * BX, BX), 0)
            - BX // 2
            - lax.broadcasted_iota(jnp.int32, (2 * BX, BX), 1)
        ),
        0,
    ).astype(F32).astype(jnp.bfloat16)
    padded[:, :, : BX // 2] = jnp.zeros((depth, span, BX // 2), F32)
    padded[:, :, extent + BX // 2 :] = jnp.zeros((depth, span, BX // 2), F32)

    def remote(src, dst, ssem, rsem, axis, step):
        return pltpu.make_async_remote_copy(
            src_ref=src, dst_ref=dst, send_sem=ssem, recv_sem=rsem,
            device_id=peer(axis, step), device_id_type=MESH,
        )

    def y_copy(item, g, side):
        rows = pl.ds(g * GROUP, GROUP)
        return remote(
            y_send.at[item, side, rows], y_recv.at[item, side, rows],
            y_ssem.at[item, g, side], y_rsem.at[item, g, side],
            "blk", 1 if side == 0 else -1,
        )

    def by_corner(item, g):
        return n_blk == 4 and (item == 1 or (item >= 2 and g == groups - 1))

    def to_corner(item, g, side):
        rows = pl.ds(g * GROUP, GROUP)
        return remote(
            y_send.at[item, side, rows], passing.at[item, rows],
            pass_ssem.at[item, g], pass_rsem.at[item, g],
            "blk", 2 if side == 0 else -2,
        )

    def from_corner(item, g, side):
        rows = pl.ds(g * GROUP, GROUP)
        return remote(
            passing.at[item, rows], y_recv.at[item, side, rows],
            onward_ssem.at[item, g], y_rsem.at[item, g, side],
            "blk", -1 if side == 0 else 1,
        )

    def y_out(item, g, act):
        for side, sign in ((0, 1), (1, -1)):
            where = has("blk", sign)
            if by_corner(item, g):
                source = blk == (1 if side == 0 else 2)
                where = jnp.logical_and(where, jnp.logical_not(source))

                @pl.when(source)
                def _(side=side):
                    copy = to_corner(item, g, side)
                    copy.start() if act == "start" else copy.wait_send()

            @pl.when(where)
            def _(side=side):
                copy = y_copy(item, g, side)
                copy.start() if act == "start" else copy.wait_send()

    def corner(item, g, act):
        if not by_corner(item, g):
            return
        for side, at in ((0, 3), (1, 0)):

            @pl.when(blk == at)
            def _(side=side):
                if act == "start":
                    to_corner(item, g, side).wait_recv()
                    from_corner(item, g, side).start()
                else:
                    from_corner(item, g, side).wait_send()

    def z_copy(item, buf, side):
        src, dst = (depth, 0) if side == 0 else (1, depth + 1)
        return remote(
            buf.at[src], buf.at[dst], z_ssem.at[item, side], z_rsem.at[item, side],
            "grp", 1 if side == 0 else -1,
        )

    def mom_copy(k, g, side):
        rows = pl.ds(g * GROUP, GROUP)
        return remote(
            mom_send.at[:, rows], mom_recv.at[k, side, :, rows],
            mom_ssem.at[k, g, side], mom_rsem.at[k, g, side],
            "blk", near[k] if side == 0 else -near[k],
        )

    def far_y_copy(k, g, side):
        rows = pl.ds(g * GROUP, GROUP)
        return remote(
            raw.at[rows], refs[43].at[k, side, rows],
            refs[44].at[k, g, side], refs[45].at[k, g, side],
            "blk", far[k] if side == 0 else -far[k],
        )

    def far_z_copy(g, side):
        rows = pl.ds(g * GROUP, GROUP)
        return remote(
            filt.at[rows], far_z.at[side, rows], fz_ssem.at[g, side], fz_rsem.at[g, side],
            "grp", 2 if side == 0 else -2,
        )

    def zmom_copy(side):
        return remote(
            zmom_send, zmom_recv.at[side], zm_ssem.at[side], zm_rsem.at[side],
            "grp", 1 if side == 0 else -1,
        )

    def both(make, axis, step, act):
        for side, sign in ((0, 1), (1, -1)):
            where = has(axis, -sign * step) if act == "come" else has(axis, sign * step)

            @pl.when(where)
            def _(side=side):
                copy = make(side)
                if act == "start":
                    copy.start()
                elif act == "sent":
                    copy.wait_send()
                else:
                    copy.wait_recv()

    def one(make, axis, step, side, act):
        sign = 1 if side == 0 else -1
        where = has(axis, -sign * step) if act == "come" else has(axis, sign * step)

        @pl.when(where)
        def _():
            copy = make(side)
            if act == "start":
                copy.start()
            elif act == "sent":
                copy.wait_send()
            else:
                copy.wait_recv()

    def x_shift(v):
        low = jnp.where(lane == 0, 0.0, pltpu.roll(v, 1, 1))
        high = jnp.where(lane == extent - 1, 0.0, pltpu.roll(v, extent - 1, 1))
        return low, high

    def y_shift(v, low_row, high_row):
        low = jnp.where(row == 0, low_row, pltpu.roll(v, 1, 0))
        high = jnp.where(row == span - 1, high_row, pltpu.roll(v, span - 1, 0))
        return low, high

    def halo(item, z):
        return y_recv[item, 0, pl.ds(z, 1), :], y_recv[item, 1, pl.ds(z, 1), :]

    def put_rows(item, z, v):
        y_send[item, 0, pl.ds(z, 1), :] = v[span - 1 : span]
        y_send[item, 1, pl.ds(z, 1), :] = v[0:1]

    def layers(g, body):
        @pl.loop(g * GROUP, (g + 1) * GROUP)
        def _(z):
            body(z)

    loads[0].wait()
    loads[1].wait()

    def conductivity(z):
        s = solid[z]
        c = COND_FLOOR + (1.0 - COND_FLOOR) * (s * s * s)
        cond[z + 1] = c
        put_rows(0, z, c)
        put_rows(1, z, temp[z + 1])

    pl.semaphore_wait(barrier, total)
    for g in range(groups):
        layers(g, conductivity)
        y_out(0, g, "start")
        if g == 0:
            one(functools.partial(z_copy, 0, cond), "grp", 1, 1, "start")
    one(functools.partial(z_copy, 0, cond), "grp", 1, 0, "start")
    loads[2].wait()
    loads[3].wait()

    def start_adjoint(z):
        c = cond[z + 1]
        low_row, high_row = halo(0, z)
        xl, xh = x_shift(c)
        yl, yh = y_shift(c, low_row, high_row)
        near_sum = (cond[z] + cond[z + 2]) + (xl + xh) + (yl + yh)
        inverse = 1.0 / (coupling[z] + 3.0 * c + 0.5 * near_sum)
        a = target[z] * inverse
        third[z] = inverse * (1.0 / 3.0)
        fixed[z] = a * (2.0 / 3.0)
        adj[0, z + 1] = a
        put_rows(2, z, a)

    def sweep(s, z):
        c = cond[z + 1]
        a = adj[s, z + 1]
        cl, ch = halo(0, z)
        al, ah = halo(s + 2, z)
        ca = c * a
        axl, axh = x_shift(a)
        gxl, gxh = x_shift(ca)
        ayl, ayh = y_shift(a, al, ah)
        gyl, gyh = y_shift(ca, cl * al, ch * ah)
        below, above = adj[s, z], adj[s, z + 2]
        plain = (below + above) + (axl + axh) + (ayl + ayh)
        weighted = (cond[z] * below + cond[z + 2] * above) + (gxl + gxh) + (gyl + gyh)
        new = a * (1.0 / 3.0) + fixed[z] + third[z] * (c * plain + weighted)
        adj[s + 1, z + 1] = new
        put_rows(s + 3, z, new)

    def raw_terms(z):
        a = adj[SWEEPS, z + 1]
        t = temp[z + 1]
        al, ah = halo(SWEEPS + 2, z)
        tl, th = halo(1, z)
        axl, axh = x_shift(a)
        txl, txh = x_shift(t)
        ayl, ayh = y_shift(a, al, ah)
        tyl, tyh = y_shift(t, tl, th)
        total_terms = (
            (a - adj[SWEEPS, z]) * (t - temp[z])
            + (a - adj[SWEEPS, z + 2]) * (t - temp[z + 2])
            + (a - axl) * (t - txl)
            + (a - axh) * (t - txh)
            + (a - ayl) * (t - tyl)
            + (a - ayh) * (t - tyh)
        )
        s = solid[z]
        value = total_terms * (s * s) * scale[...] * z_inv[pl.ds(z, 1), :]
        raw[z] = value
        mom_send[0, pl.ds(z, 1), :] = jnp.sum(value, axis=0, keepdims=True)
        mom_send[1, pl.ds(z, 1), :] = jnp.sum(value * row_f, axis=0, keepdims=True)

    def stage(item, buf, body, wait_item, wait_buf, after):
        for g in range(groups):
            both(functools.partial(y_copy, wait_item, g), "blk", 1, "come")
            if wait_item == SWEEPS + 2:
                both(functools.partial(y_copy, 1, g), "blk", 1, "come")
            if g == 0:
                one(functools.partial(z_copy, wait_item, wait_buf), "grp", 1, 0, "come")
                if wait_item == SWEEPS + 2:
                    one(functools.partial(z_copy, 1, temp), "grp", 1, 0, "come")
            if g == groups - 1:
                one(functools.partial(z_copy, wait_item, wait_buf), "grp", 1, 1, "come")
                if wait_item == SWEEPS + 2:
                    one(functools.partial(z_copy, 1, temp), "grp", 1, 1, "come")
            layers(g, body)
            if g == 0:
                corner(wait_item, groups - 1, "start")
                if wait_item == 3:
                    for part in range(groups):
                        corner(1, part, "start")
            if item is None:
                after(g)
            else:
                y_out(item, g, "start")
                if g == 0:
                    one(functools.partial(z_copy, item, buf), "grp", 1, 1, "start")
        if item is not None:
            one(functools.partial(z_copy, item, buf), "grp", 1, 0, "start")

    stage(2, adj.at[0], start_adjoint, 0, cond, None)
    for g in range(groups):
        y_out(1, g, "start")
    both(functools.partial(z_copy, 1, temp), "grp", 1, "start")
    for s in range(SWEEPS):
        stage(s + 3, adj.at[s + 1], functools.partial(sweep, s), s + 2, adj.at[s], None)

    def send_moments(g):
        for k, d in enumerate(near):
            both(functools.partial(mom_copy, k, g), "blk", d, "start")
        for k, d in enumerate(far):
            both(functools.partial(far_y_copy, k, g), "blk", d, "start")

    stage(None, None, raw_terms, SWEEPS + 2, adj.at[SWEEPS], send_moments)

    zmom_send[...] = jnp.zeros((2, span, extent), F32)

    def along_y(z):
        level = jnp.zeros((1, extent), F32)
        slope = jnp.zeros((1, extent), F32)
        for k, d in enumerate(near):
            weight = float(RADIUS + 1 - span * d)
            low0, low1 = mom_recv[k, 0, 0, pl.ds(z, 1), :], mom_recv[k, 0, 1, pl.ds(z, 1), :]
            high0, high1 = mom_recv[k, 1, 0, pl.ds(z, 1), :], mom_recv[k, 1, 1, pl.ds(z, 1), :]
            level = level + weight * (low0 + high0) + (low1 - high1)
            slope = slope + (high0 - low0)
        value = level + slope * row_f
        here = raw[z]
        for i in range(span):
            value = value + (RADIUS + 1 - jnp.abs(row - i)).astype(F32) * here[i : i + 1]
        for k, d in enumerate(far):
            low, high = refs[43][k, 0, z], refs[43][k, 1, z]
            for i in range(span):
                w_low = jnp.maximum(RADIUS + 1 - (span * d + row - i), 0).astype(F32)
                w_high = jnp.maximum(RADIUS + 1 - (span * d + i - row), 0).astype(F32)
                value = value + w_low * low[i : i + 1] + w_high * high[i : i + 1]
        filt[z] = value
        zmom_send[0] += value
        zmom_send[1] += value * jnp.asarray(z, F32)

    for g in range(groups):
        for k, d in enumerate(near):
            both(functools.partial(mom_copy, k, g), "blk", d, "come")
        for k, d in enumerate(far):
            both(functools.partial(far_y_copy, k, g), "blk", d, "come")
        layers(g, along_y)
        both(functools.partial(far_z_copy, g), "grp", 2, "start")
    both(zmom_copy, "grp", 1, "start")
    both(zmom_copy, "grp", 1, "come")
    for g in range(groups):
        both(functools.partial(far_z_copy, g), "grp", 2, "come")

    width = 512

    @pl.loop(0, extent // width)
    def _(b):
        cols = pl.ds(pl.multiple_of(b * width, width), width)
        shifted = pl.ds(pl.multiple_of(b * width + BX // 2, 128), width)
        own0, own1 = zmom_send[0, :, cols], zmom_send[1, :, cols]
        low0, low1 = zmom_recv[0, 0, :, cols], zmom_recv[0, 1, :, cols]
        high0, high1 = zmom_recv[1, 0, :, cols], zmom_recv[1, 1, :, cols]
        weight = float(RADIUS + 1 - depth)
        level = (RADIUS + 1.0) * own0 - own1 + weight * (low0 + high0) + low1 - high1
        slope = own0 - low0 + high0
        zero = jnp.zeros((span, width), F32)

        def up(z, carry):
            line, twice, once, far_twice, far_once = carry
            far_once = far_once + far_z[1, z, :, cols]
            far_twice = far_twice + far_once
            padded[z, :, shifted] = line - 2.0 * twice + far_twice
            once = once + filt[z, :, cols]
            return line + slope, twice + once, once, far_twice, far_once

        lax.fori_loop(0, depth, up, (level, zero, zero, zero, zero))

        def down(k, carry):
            far_twice, far_once = carry
            z = depth - 1 - k
            far_once = far_once + far_z[0, z, :, cols]
            far_twice = far_twice + far_once
            padded[z, :, shifted] += far_twice
            return far_twice, far_once

        lax.fori_loop(0, depth, down, (zero, zero))

    @pl.loop(0, extent // BX)
    def _(b):
        window = padded[:, :, pl.ds(pl.multiple_of(b * BX, BX), 2 * BX)]
        window = window.reshape(depth * span, 2 * BX)
        high = window.astype(jnp.bfloat16)
        low = (window - high.astype(F32)).astype(jnp.bfloat16)
        weights = cone[...]
        product = jnp.dot(high, weights, preferred_element_type=F32) + jnp.dot(
            low, weights, preferred_element_type=F32
        )
        cols = pl.ds(pl.multiple_of(b * BX, BX), BX)
        out[:, :, cols] = product.reshape(depth, span, BX) * (
            REPORT_SCALE * mask[:, cols]
        )

    for item in range(SWEEPS + 3):
        for g in range(groups):
            y_out(item, g, "sent")
            corner(item, g, "sent")
        buf = (cond, temp)[item] if item < 2 else adj.at[item - 2]
        both(functools.partial(z_copy, item, buf), "grp", 1, "sent")
    for g in range(groups):
        for k, d in enumerate(near):
            both(functools.partial(mom_copy, k, g), "blk", d, "sent")
        for k, d in enumerate(far):
            both(functools.partial(far_y_copy, k, g), "blk", d, "sent")
        both(functools.partial(far_z_copy, g), "grp", 2, "sent")
    both(zmom_copy, "grp", 1, "sent")


def local(n_grp, n_blk, solid, temp, target, coupling, switch):
    depth, span, extent = solid.shape
    groups = depth // GROUP
    assert 2 * depth == RADIUS and depth % GROUP == 0
    near, far = [], []
    for d in range(1, n_blk):
        if (d + 1) * span - 1 <= RADIUS + 1:
            near.append(d)
        elif (d - 1) * span + 1 <= RADIUS:
            far.append(d)
    items = SWEEPS + 3
    block = (depth, span, extent)
    framed = (depth + 2, span, extent)
    vmem = lambda *shape: pltpu.VMEM(shape, F32)
    dma = lambda *shape: pltpu.SemaphoreType.DMA(shape)
    scratch = [
        vmem(*block), vmem(*framed), vmem(*block), vmem(*block),
        vmem(*framed), vmem(SWEEPS + 1, *framed), vmem(*block), vmem(*block),
        vmem(*block), vmem(*block),
        vmem(items, 2, depth, extent), vmem(items, 2, depth, extent),
        vmem(2, depth, extent), vmem(len(near), 2, 2, depth, extent),
        vmem(2, span, extent), vmem(2, 2, span, extent), vmem(2, *block),
        vmem(span, extent), vmem(span, extent), vmem(depth, extent),
        vmem(depth, span, extent + BX), pltpu.VMEM((2 * BX, BX), jnp.bfloat16),
        dma(4), dma(items, groups, 2), dma(items, groups, 2), dma(items, 2), dma(items, 2),
        dma(len(near), groups, 2), dma(len(near), groups, 2), dma(2), dma(2),
        dma(groups, 2), dma(groups, 2),
        vmem(items, depth, extent), dma(items, groups), dma(items, groups), dma(items, groups),
    ]
    if far:
        scratch += [
            vmem(len(far), 2, *block), dma(len(far), groups, 2), dma(len(far), groups, 2),
        ]
    return pl.pallas_call(
        functools.partial(kernel, n_grp, n_blk, near, far),
        out_shape=jax.ShapeDtypeStruct(block, F32),
        in_specs=[pl.BlockSpec(memory_space=pl.ANY)] * 4
        + [pl.BlockSpec(memory_space=pltpu.SMEM)],
        out_specs=pl.BlockSpec(memory_space=pltpu.VMEM),
        scratch_shapes=scratch,
        compiler_params=pltpu.CompilerParams(
            collective_id=0, has_side_effects=True, vmem_limit_bytes=60 * 2**20
        ),
        cost_estimate=pl.CostEstimate(
            flops=2 * 10**9, bytes_accessed=8 * 10**6, transcendentals=0
        ),
    )(solid, temp, target, coupling, switch)


def solution(mesh):
    spec = P("grp", "blk", None)
    return jax.shard_map(
        functools.partial(local, mesh.shape["grp"], mesh.shape["blk"]),
        mesh=mesh,
        in_specs=(spec,) * 5,
        out_specs=spec,
        check_vma=False,
    )
```

```python
import functools

import jax
import jax.numpy as jnp
from jax import lax
from jax.experimental import pallas as pl
from jax.experimental.pallas import tpu as pltpu
from jax.sharding import PartitionSpec as P

BX = 256
RADIUS = 48
SWEEPS = 4
COND_FLOOR = 0.001
REPORT_SCALE = 100.0
GROUP = 8

MESH = pl.DeviceIdType.MESH
F32 = jnp.float32


def coverage(position, length):
    low = jnp.maximum(RADIUS - position, 0)
    high = jnp.maximum(RADIUS - (length - 1 - position), 0)
    lost = low * (low + 1) // 2 + high * (high + 1) // 2
    return ((RADIUS + 1) ** 2 - lost).astype(F32)


def kernel(n_grp, n_blk, near, far, *refs):
    (
        solid_hbm, temp_hbm, target_hbm, coupling_hbm, switch,
        padded,
        solid, temp, target, coupling, cond, adj, third, fixed, raw, filt,
        y_send, y_recv, mom_send, mom_recv, zmom_send, zmom_recv, far_z,
        mask, scale, z_inv,
        load_sem, y_ssem, y_rsem, z_ssem, z_rsem,
        mom_ssem, mom_rsem, zm_ssem, zm_rsem, fz_ssem, fz_rsem,
        passing, pass_ssem, pass_rsem, onward_ssem,
    ) = refs[:41]
    depth, span, extent = solid.shape
    groups = depth // GROUP
    grp = lax.axis_index("grp")
    blk = lax.axis_index("blk")
    reach = max(near + far)

    def has(axis, step):
        if axis == "grp":
            at, count = grp + step, n_grp
        else:
            at, count = blk + step, n_blk
        return (at < count) if step > 0 else (at >= 0)

    def peer(axis, step):
        return {axis: (grp if axis == "grp" else blk) + step}

    partners = [("grp", s * d) for d in (1, 2) for s in (1, -1) if d < n_grp]
    partners += [("blk", s * d) for d in near + far for s in (1, -1)]

    loads = [
        pltpu.make_async_copy(solid_hbm, solid, load_sem.at[0]),
        pltpu.make_async_copy(temp_hbm, temp.at[pl.ds(1, depth)], load_sem.at[1]),
        pltpu.make_async_copy(target_hbm, target, load_sem.at[2]),
        pltpu.make_async_copy(coupling_hbm, coupling, load_sem.at[3]),
    ]
    for load in loads:
        load.start()

    barrier = pltpu.get_barrier_semaphore()
    total = 0
    for axis, step in partners:
        total = total + has(axis, step).astype(jnp.int32)

        @pl.when(has(axis, step))
        def _(axis=axis, step=step):
            pl.semaphore_signal(
                barrier, inc=1, device_id=peer(axis, step), device_id_type=MESH
            )

    for side, step in ((0, -1), (1, 1)):
        edge = 0 if side == 0 else depth + 1

        @pl.when(jnp.logical_not(has("grp", step)))
        def _(side=side, edge=edge):
            zero = jnp.zeros((span, extent), F32)
            cond[edge] = zero
            temp[edge] = zero
            for s in range(SWEEPS + 1):
                adj[s, edge] = zero
            zmom_recv[side] = jnp.zeros((2, span, extent), F32)

        @pl.when(jnp.logical_not(has("grp", 2 * step)))
        def _(side=side):
            far_z[side] = jnp.zeros((depth, span, extent), F32)

        @pl.when(jnp.logical_not(has("blk", step)))
        def _(side=side):
            for item in range(SWEEPS + 3):
                y_recv[item, side] = jnp.zeros((depth, extent), F32)

        for k, d in enumerate(near):

            @pl.when(jnp.logical_not(has("blk", d * step)))
            def _(side=side, k=k):
                mom_recv[k, side] = jnp.zeros((2, depth, extent), F32)

        for k, d in enumerate(far):

            @pl.when(jnp.logical_not(has("blk", d * step)))
            def _(side=side, k=k):
                refs[41][k, side] = jnp.zeros((depth, span, extent), F32)

    row = lax.broadcasted_iota(jnp.int32, (span, extent), 0)
    lane = lax.broadcasted_iota(jnp.int32, (span, extent), 1)
    row_f = row.astype(F32)

    for b in range(extent // BX):
        mask[:, b * BX : (b + 1) * BX] = jnp.full(
            (span, BX), switch[0, 0, b].astype(F32), F32
        )
    scale[...] = (
        mask[...]
        * (-1.5 * (1.0 - COND_FLOOR))
        / (coverage(lane, extent) * coverage(row + blk * span, span * n_blk))
    )
    z_inv[...] = 1.0 / coverage(
        lax.broadcasted_iota(jnp.int32, (depth, extent), 0) + grp * depth, depth * n_grp
    )
    padded[:, :, : BX // 2] = jnp.zeros((depth, span, BX // 2), F32)
    padded[:, :, extent + BX // 2 :] = jnp.zeros((depth, span, BX // 2), F32)

    def remote(src, dst, ssem, rsem, axis, step):
        return pltpu.make_async_remote_copy(
            src_ref=src, dst_ref=dst, send_sem=ssem, recv_sem=rsem,
            device_id=peer(axis, step), device_id_type=MESH,
        )

    def y_copy(item, g, side):
        rows = pl.ds(g * GROUP, GROUP)
        return remote(
            y_send.at[item, side, rows], y_recv.at[item, side, rows],
            y_ssem.at[item, g, side], y_rsem.at[item, g, side],
            "blk", 1 if side == 0 else -1,
        )

    def by_corner(item, g):
        return n_blk == 4 and (item == 1 or g == groups - 1)

    def to_corner(item, g, side):
        rows = pl.ds(g * GROUP, GROUP)
        return remote(
            y_send.at[item, side, rows], passing.at[item, rows],
            pass_ssem.at[item, g], pass_rsem.at[item, g],
            "blk", 2 if side == 0 else -2,
        )

    def from_corner(item, g, side):
        rows = pl.ds(g * GROUP, GROUP)
        return remote(
            passing.at[item, rows], y_recv.at[item, side, rows],
            onward_ssem.at[item, g], y_rsem.at[item, g, side],
            "blk", -1 if side == 0 else 1,
        )

    def y_out(item, g, act):
        for side, sign in ((0, 1), (1, -1)):
            where = has("blk", sign)
            if by_corner(item, g):
                source = blk == (1 if side == 0 else 2)
                where = jnp.logical_and(where, jnp.logical_not(source))

                @pl.when(source)
                def _(side=side):
                    copy = to_corner(item, g, side)
                    copy.start() if act == "start" else copy.wait_send()

            @pl.when(where)
            def _(side=side):
                copy = y_copy(item, g, side)
                copy.start() if act == "start" else copy.wait_send()

    def corner(item, g, act):
        if not by_corner(item, g):
            return
        for side, at in ((0, 3), (1, 0)):

            @pl.when(blk == at)
            def _(side=side):
                if act == "start":
                    to_corner(item, g, side).wait_recv()
                    from_corner(item, g, side).start()
                else:
                    from_corner(item, g, side).wait_send()

    def z_copy(item, buf, side):
        src, dst = (depth, 0) if side == 0 else (1, depth + 1)
        return remote(
            buf.at[src], buf.at[dst], z_ssem.at[item, side], z_rsem.at[item, side],
            "grp", 1 if side == 0 else -1,
        )

    def mom_copy(k, g, side):
        rows = pl.ds(g * GROUP, GROUP)
        return remote(
            mom_send.at[:, rows], mom_recv.at[k, side, :, rows],
            mom_ssem.at[k, g, side], mom_rsem.at[k, g, side],
            "blk", near[k] if side == 0 else -near[k],
        )

    def far_y_copy(k, g, side):
        rows = pl.ds(g * GROUP, GROUP)
        return remote(
            raw.at[rows], refs[41].at[k, side, rows],
            refs[42].at[k, g, side], refs[43].at[k, g, side],
            "blk", far[k] if side == 0 else -far[k],
        )

    def far_z_copy(g, side):
        rows = pl.ds(g * GROUP, GROUP)
        return remote(
            filt.at[rows], far_z.at[side, rows], fz_ssem.at[g, side], fz_rsem.at[g, side],
            "grp", 2 if side == 0 else -2,
        )

    def zmom_copy(side):
        return remote(
            zmom_send, zmom_recv.at[side], zm_ssem.at[side], zm_rsem.at[side],
            "grp", 1 if side == 0 else -1,
        )

    def both(make, axis, step, act):
        for side, sign in ((0, 1), (1, -1)):
            where = has(axis, -sign * step) if act == "come" else has(axis, sign * step)

            @pl.when(where)
            def _(side=side):
                copy = make(side)
                if act == "start":
                    copy.start()
                elif act == "sent":
                    copy.wait_send()
                else:
                    copy.wait_recv()

    def one(make, axis, step, side, act):
        sign = 1 if side == 0 else -1
        where = has(axis, -sign * step) if act == "come" else has(axis, sign * step)

        @pl.when(where)
        def _():
            copy = make(side)
            if act == "start":
                copy.start()
            elif act == "sent":
                copy.wait_send()
            else:
                copy.wait_recv()

    def x_shift(v):
        low = jnp.where(lane == 0, 0.0, pltpu.roll(v, 1, 1))
        high = jnp.where(lane == extent - 1, 0.0, pltpu.roll(v, extent - 1, 1))
        return low, high

    def y_shift(v, low_row, high_row):
        low = jnp.where(row == 0, low_row, pltpu.roll(v, 1, 0))
        high = jnp.where(row == span - 1, high_row, pltpu.roll(v, span - 1, 0))
        return low, high

    def halo(item, z):
        return y_recv[item, 0, pl.ds(z, 1), :], y_recv[item, 1, pl.ds(z, 1), :]

    def put_rows(item, z, v):
        y_send[item, 0, pl.ds(z, 1), :] = v[span - 1 : span]
        y_send[item, 1, pl.ds(z, 1), :] = v[0:1]

    def layers(g, body):
        @pl.loop(g * GROUP, (g + 1) * GROUP)
        def _(z):
            body(z)

    loads[0].wait()
    loads[1].wait()

    def conductivity(z):
        s = solid[z]
        c = COND_FLOOR + (1.0 - COND_FLOOR) * (s * s * s)
        cond[z + 1] = c
        put_rows(0, z, c)
        put_rows(1, z, temp[z + 1])

    pl.semaphore_wait(barrier, total)
    for g in range(groups):
        layers(g, conductivity)
        y_out(0, g, "start")
        if g == 0:
            one(functools.partial(z_copy, 0, cond), "grp", 1, 1, "start")
    one(functools.partial(z_copy, 0, cond), "grp", 1, 0, "start")
    loads[2].wait()
    loads[3].wait()

    def start_adjoint(z):
        c = cond[z + 1]
        low_row, high_row = halo(0, z)
        xl, xh = x_shift(c)
        yl, yh = y_shift(c, low_row, high_row)
        near_sum = (cond[z] + cond[z + 2]) + (xl + xh) + (yl + yh)
        inverse = 1.0 / (coupling[z] + 3.0 * c + 0.5 * near_sum)
        a = target[z] * inverse
        third[z] = inverse * (1.0 / 3.0)
        fixed[z] = a * (2.0 / 3.0)
        adj[0, z + 1] = a
        put_rows(2, z, a)

    def sweep(s, z):
        c = cond[z + 1]
        a = adj[s, z + 1]
        cl, ch = halo(0, z)
        al, ah = halo(s + 2, z)
        ca = c * a
        axl, axh = x_shift(a)
        gxl, gxh = x_shift(ca)
        ayl, ayh = y_shift(a, al, ah)
        gyl, gyh = y_shift(ca, cl * al, ch * ah)
        below, above = adj[s, z], adj[s, z + 2]
        plain = (below + above) + (axl + axh) + (ayl + ayh)
        weighted = (cond[z] * below + cond[z + 2] * above) + (gxl + gxh) + (gyl + gyh)
        new = a * (1.0 / 3.0) + fixed[z] + third[z] * (c * plain + weighted)
        adj[s + 1, z + 1] = new
        put_rows(s + 3, z, new)

    def raw_terms(z):
        a = adj[SWEEPS, z + 1]
        t = temp[z + 1]
        al, ah = halo(SWEEPS + 2, z)
        tl, th = halo(1, z)
        axl, axh = x_shift(a)
        txl, txh = x_shift(t)
        ayl, ayh = y_shift(a, al, ah)
        tyl, tyh = y_shift(t, tl, th)
        total_terms = (
            (a - adj[SWEEPS, z]) * (t - temp[z])
            + (a - adj[SWEEPS, z + 2]) * (t - temp[z + 2])
            + (a - axl) * (t - txl)
            + (a - axh) * (t - txh)
            + (a - ayl) * (t - tyl)
            + (a - ayh) * (t - tyh)
        )
        s = solid[z]
        value = total_terms * (s * s) * scale[...] * z_inv[pl.ds(z, 1), :]
        raw[z] = value
        mom_send[0, pl.ds(z, 1), :] = jnp.sum(value, axis=0, keepdims=True)
        mom_send[1, pl.ds(z, 1), :] = jnp.sum(value * row_f, axis=0, keepdims=True)

    def stage(item, buf, body, wait_item, wait_buf, after):
        for g in range(groups):
            both(functools.partial(y_copy, wait_item, g), "blk", 1, "come")
            if wait_item == SWEEPS + 2:
                both(functools.partial(y_copy, 1, g), "blk", 1, "come")
            if g == 0:
                one(functools.partial(z_copy, wait_item, wait_buf), "grp", 1, 0, "come")
                if wait_item == SWEEPS + 2:
                    one(functools.partial(z_copy, 1, temp), "grp", 1, 0, "come")
            if g == groups - 1:
                one(functools.partial(z_copy, wait_item, wait_buf), "grp", 1, 1, "come")
                if wait_item == SWEEPS + 2:
                    one(functools.partial(z_copy, 1, temp), "grp", 1, 1, "come")
            layers(g, body)
            if g == 0:
                corner(wait_item, groups - 1, "start")
                if wait_item == 3:
                    for part in range(groups):
                        corner(1, part, "start")
            if item is None:
                after(g)
            else:
                y_out(item, g, "start")
                if g == 0:
                    one(functools.partial(z_copy, item, buf), "grp", 1, 1, "start")
        if item is not None:
            one(functools.partial(z_copy, item, buf), "grp", 1, 0, "start")

    stage(2, adj.at[0], start_adjoint, 0, cond, None)
    for g in range(groups):
        y_out(1, g, "start")
    both(functools.partial(z_copy, 1, temp), "grp", 1, "start")
    for s in range(SWEEPS):
        stage(s + 3, adj.at[s + 1], functools.partial(sweep, s), s + 2, adj.at[s], None)

    def send_moments(g):
        for k, d in enumerate(near):
            both(functools.partial(mom_copy, k, g), "blk", d, "start")
        for k, d in enumerate(far):
            both(functools.partial(far_y_copy, k, g), "blk", d, "start")

    stage(None, None, raw_terms, SWEEPS + 2, adj.at[SWEEPS], send_moments)

    zmom_send[...] = jnp.zeros((2, span, extent), F32)

    def along_y(z):
        level = jnp.zeros((1, extent), F32)
        slope = jnp.zeros((1, extent), F32)
        for k, d in enumerate(near):
            weight = float(RADIUS + 1 - span * d)
            low0, low1 = mom_recv[k, 0, 0, pl.ds(z, 1), :], mom_recv[k, 0, 1, pl.ds(z, 1), :]
            high0, high1 = mom_recv[k, 1, 0, pl.ds(z, 1), :], mom_recv[k, 1, 1, pl.ds(z, 1), :]
            level = level + weight * (low0 + high0) + (low1 - high1)
            slope = slope + (high0 - low0)
        value = level + slope * row_f
        here = raw[z]
        for i in range(span):
            value = value + (RADIUS + 1 - jnp.abs(row - i)).astype(F32) * here[i : i + 1]
        for k, d in enumerate(far):
            low, high = refs[41][k, 0, z], refs[41][k, 1, z]
            for i in range(span):
                w_low = jnp.maximum(RADIUS + 1 - (span * d + row - i), 0).astype(F32)
                w_high = jnp.maximum(RADIUS + 1 - (span * d + i - row), 0).astype(F32)
                value = value + w_low * low[i : i + 1] + w_high * high[i : i + 1]
        filt[z] = value
        zmom_send[0] += value
        zmom_send[1] += value * jnp.asarray(z, F32)

    for g in range(groups):
        for k, d in enumerate(near):
            both(functools.partial(mom_copy, k, g), "blk", d, "come")
        for k, d in enumerate(far):
            both(functools.partial(far_y_copy, k, g), "blk", d, "come")
        layers(g, along_y)
        both(functools.partial(far_z_copy, g), "grp", 2, "start")
    both(zmom_copy, "grp", 1, "start")
    both(zmom_copy, "grp", 1, "come")
    for g in range(groups):
        both(functools.partial(far_z_copy, g), "grp", 2, "come")

    width = 512

    @pl.loop(0, extent // width)
    def _(b):
        cols = pl.ds(pl.multiple_of(b * width, width), width)
        shifted = pl.ds(pl.multiple_of(b * width + BX // 2, 128), width)
        own0, own1 = zmom_send[0, :, cols], zmom_send[1, :, cols]
        low0, low1 = zmom_recv[0, 0, :, cols], zmom_recv[0, 1, :, cols]
        high0, high1 = zmom_recv[1, 0, :, cols], zmom_recv[1, 1, :, cols]
        weight = float(RADIUS + 1 - depth)
        level = (RADIUS + 1.0) * own0 - own1 + weight * (low0 + high0) + low1 - high1
        slope = own0 - low0 + high0
        zero = jnp.zeros((span, width), F32)

        def up(z, carry):
            line, twice, once, far_twice, far_once = carry
            far_once = far_once + far_z[1, z, :, cols]
            far_twice = far_twice + far_once
            padded[z, :, shifted] = line - 2.0 * twice + far_twice
            once = once + filt[z, :, cols]
            return line + slope, twice + once, once, far_twice, far_once

        lax.fori_loop(0, depth, up, (level, zero, zero, zero, zero))

        def down(k, carry):
            far_twice, far_once = carry
            z = depth - 1 - k
            far_once = far_once + far_z[0, z, :, cols]
            far_twice = far_twice + far_once
            padded[z, :, shifted] += far_twice
            return far_twice, far_once

        lax.fori_loop(0, depth, down, (zero, zero))

    for item in range(SWEEPS + 3):
        for g in range(groups):
            y_out(item, g, "sent")
            corner(item, g, "sent")
        buf = (cond, temp)[item] if item < 2 else adj.at[item - 2]
        both(functools.partial(z_copy, item, buf), "grp", 1, "sent")
    for g in range(groups):
        for k, d in enumerate(near):
            both(functools.partial(mom_copy, k, g), "blk", d, "sent")
        for k, d in enumerate(far):
            both(functools.partial(far_y_copy, k, g), "blk", d, "sent")
        both(functools.partial(far_z_copy, g), "grp", 2, "sent")
    both(zmom_copy, "grp", 1, "sent")


def along_x(switch, padded, out, cone):
    depth, span, _ = out.shape
    b = pl.program_id(0)

    @pl.when(b == 0)
    def _():
        distance = (
            lax.broadcasted_iota(jnp.int32, (2 * BX, BX), 0)
            - BX // 2
            - lax.broadcasted_iota(jnp.int32, (2 * BX, BX), 1)
        )
        weights = jnp.maximum(RADIUS + 1 - jnp.abs(distance), 0)
        cone[...] = weights.astype(F32).astype(jnp.bfloat16)

    window = padded[:, :, pl.ds(pl.multiple_of(b * BX, BX), 2 * BX)]
    window = window.reshape(depth * span, 2 * BX)
    high = window.astype(jnp.bfloat16)
    low = (window - high.astype(F32)).astype(jnp.bfloat16)
    weights = cone[...]
    product = jnp.dot(high, weights, preferred_element_type=F32) + jnp.dot(
        low, weights, preferred_element_type=F32
    )
    out[...] = product.reshape(depth, span, BX) * (
        REPORT_SCALE * switch[0, 0, b].astype(F32)
    )


def local(n_grp, n_blk, solid, temp, target, coupling, switch):
    depth, span, extent = solid.shape
    groups = depth // GROUP
    assert 2 * depth == RADIUS and depth % GROUP == 0
    near, far = [], []
    for d in range(1, n_blk):
        if (d + 1) * span - 1 <= RADIUS + 1:
            near.append(d)
        elif (d - 1) * span + 1 <= RADIUS:
            far.append(d)
    items = SWEEPS + 3
    block = (depth, span, extent)
    framed = (depth + 2, span, extent)
    vmem = lambda *shape: pltpu.VMEM(shape, F32)
    dma = lambda *shape: pltpu.SemaphoreType.DMA(shape)
    scratch = [
        vmem(*block), vmem(*framed), vmem(*block), vmem(*block),
        vmem(*framed), vmem(SWEEPS + 1, *framed), vmem(*block), vmem(*block),
        vmem(*block), vmem(*block),
        vmem(items, 2, depth, extent), vmem(items, 2, depth, extent),
        vmem(2, depth, extent), vmem(len(near), 2, 2, depth, extent),
        vmem(2, span, extent), vmem(2, 2, span, extent), vmem(2, *block),
        vmem(span, extent), vmem(span, extent), vmem(depth, extent),
        dma(4), dma(items, groups, 2), dma(items, groups, 2), dma(items, 2), dma(items, 2),
        dma(len(near), groups, 2), dma(len(near), groups, 2), dma(2), dma(2),
        dma(groups, 2), dma(groups, 2),
        vmem(items, depth, extent), dma(items, groups), dma(items, groups), dma(items, groups),
    ]
    if far:
        scratch += [
            vmem(len(far), 2, *block), dma(len(far), groups, 2), dma(len(far), groups, 2),
        ]
    padded = pl.pallas_call(
        functools.partial(kernel, n_grp, n_blk, near, far),
        out_shape=jax.ShapeDtypeStruct((depth, span, extent + BX), F32),
        in_specs=[pl.BlockSpec(memory_space=pl.ANY)] * 4
        + [pl.BlockSpec(memory_space=pltpu.SMEM)],
        out_specs=pl.BlockSpec(memory_space=pltpu.VMEM),
        scratch_shapes=scratch,
        compiler_params=pltpu.CompilerParams(
            collective_id=0, has_side_effects=True, vmem_limit_bytes=60 * 2**20
        ),
        cost_estimate=pl.CostEstimate(
            flops=2 * 10**9, bytes_accessed=8 * 10**6, transcendentals=0
        ),
    )(solid, temp, target, coupling, switch)
    return pl.pallas_call(
        along_x,
        out_shape=jax.ShapeDtypeStruct(block, F32),
        grid=(extent // BX,),
        in_specs=[
            pl.BlockSpec(memory_space=pltpu.SMEM),
            pl.BlockSpec((depth, span, extent + BX), lambda b: (0, 0, 0)),
        ],
        out_specs=pl.BlockSpec((depth, span, BX), lambda b: (0, 0, b)),
        scratch_shapes=[pltpu.VMEM((2 * BX, BX), jnp.bfloat16)],
        compiler_params=pltpu.CompilerParams(vmem_limit_bytes=24 * 2**20),
    )(switch, padded)


def solution(mesh):
    spec = P("grp", "blk", None)
    return jax.shard_map(
        functools.partial(local, mesh.shape["grp"], mesh.shape["blk"]),
        mesh=mesh,
        in_specs=(spec,) * 5,
        out_specs=spec,
        check_vma=False,
    )
```
